128 devices in a mesh: group: 2 (over z_hi), replica: 64 (over y, z_lo, x, core).
Axes of the slice: x: 4, y: 4, z: 4 (z_hi: 2, z_lo: 2; z = z_hi * 2 + z_lo), core: 2. Of those that a mesh axis runs over, the one named last changes fastest.
Arguments:
- tokens: bfloat16 [16384, 2560], P(('group', 'replica')), may hold values from -6 to 6
- entry_gain: bfloat16 [2560], P(('group', 'replica')), may hold values from 0.25 to 1.75
- query_down: bfloat16 [2560, 768], P(('group', 'replica')), may hold values from -0.125 to 0.125
- query_gain: bfloat16 [768], P(('group', 'replica')), may hold values from 0.25 to 1.75
- query_up: bfloat16 [768, 3840], P(('group', 'replica')), may hold values from -0.21875 to 0.21875
- latent_down: bfloat16 [2560, 288], P(('group', 'replica')), may hold values from -0.125 to 0.125
- latent_gain: bfloat16 [256], P(('group', 'replica')), may hold values from 0.25 to 1.75
- latent_up: bfloat16 [256, 5120], P(('group', 'replica')), may hold values from -0.375 to 0.375
- output_weight: bfloat16 [2560, 2560], P(('group', 'replica')), may hold values from -4 to 4
- ffn_gain: bfloat16 [2560], P(('group', 'replica')), may hold values from 0.25 to 1.75
- gate_weight: bfloat16 [2560, 6400], P(('group', 'replica')), may hold values from -0.125 to 0.125
- up_weight: bfloat16 [2560, 6400], P(('group', 'replica')), may hold values from -0.125 to 0.125
- down_weight: bfloat16 [6400, 2560], P(('group', 'replica')), may hold values from -0.625 to 0.625
- cotangent: bfloat16 [16384, 2560], P(('group', 'replica')), may hold values from -6 to 6
Outputs:
- block_out: bfloat16 [16384, 2560], P(('group', 'replica'))
- tokens_grad: float32 [16384, 2560], P(('group', 'replica'))
- entry_gain_grad: float32 [2560], P(('group', 'replica'))
- query_down_grad: float32 [2560, 768], P(('group', 'replica'))
- query_gain_grad: float32 [768], P(('group', 'replica'))
- query_up_grad: float32 [768, 3840], P(('group', 'replica'))
- latent_down_grad: float32 [2560, 288], P(('group', 'replica'))
- latent_gain_grad: float32 [256], P(('group', 'replica'))
- latent_up_grad: float32 [256, 5120], P(('group', 'replica'))
- output_weight_grad: float32 [2560, 2560], P(('group', 'replica'))
- ffn_gain_grad: float32 [2560], P(('group', 'replica'))
- gate_weight_grad: float32 [2560, 6400], P(('group', 'replica'))
- up_weight_grad: float32 [2560, 6400], P(('group', 'replica'))
- down_weight_grad: float32 [6400, 2560], P(('group', 'replica'))
The draws below stay inside these ranges and needn't reach their ends.
All inputs are finite; a program needn't handle non-finite values.
Results may differ from the reference program's by a relative error of at most 0.025.
Values may be sent and summed in bfloat16 or wider, within the bound.
No kernel may reach another device: no remote copies, remote signals or barrier semaphores. Data moves between devices by JAX's collectives and lax.ppermute only.
A program may use at most 768 MiB of HBM per device.

```python
import math
import jax
import jax.numpy as jnp
from jax import lax

D = 2560
QR = 768
KVR = 256
HEADS = 40
NOPE = 64
ROPE = 32
VDIM = 64
FF = 6400
SEQ_LEN = 128
TOKENS = 16384


def shard_levels(key, shape, pieces, smallest, high):
    level = 1.0
    for axis_at, shards_of in pieces:
        draws = jax.random.uniform(jax.random.fold_in(jax.random.fold_in(key, 6), axis_at), (shards_of,), jnp.float32, smallest / len(pieces), high / len(pieces))
        level = level * jnp.repeat(jnp.exp(draws), shape[axis_at] // shards_of).reshape((-1,) + (1,) * (len(shape) - 1 - axis_at))
    return level


def scatter_about(key, extent, width, reach, split=(), held_as=jnp.bfloat16):
    values = jax.random.normal(key, extent, jnp.float32) * width
    if len(split) > 0:
        values = shard_levels(key, extent, split, -0.22, 0.18) * values
    return jnp.clip(values, min=-reach, max=reach).astype(held_as)


def setup_inputs(seed: int = 0) -> dict:
    streams_of = jax.random.split(jax.random.key(seed), 15)
    return {
        "tokens": scatter_about(streams_of[0], (TOKENS, D), 1.0, 6.0, ((0, 128),)),
        "entry_gain": jnp.clip(1.0 + 0.15 * jax.random.normal(streams_of[1], (D,), jnp.float32), 0.25, 1.75).astype(jnp.bfloat16),
        "query_down": scatter_about(streams_of[2], (D, QR), D ** -0.5, 0.125, ((0, 128),)),
        "query_gain": jnp.clip(1.0 + 0.15 * jax.random.normal(streams_of[3], (QR,), jnp.float32), 0.25, 1.75).astype(jnp.bfloat16),
        "query_up": scatter_about(streams_of[4], (QR, HEADS * (NOPE + ROPE)), QR ** -0.5, 0.21875, ((0, 128),)),
        "latent_down": scatter_about(streams_of[5], (D, KVR + ROPE), D ** -0.5, 0.125, ((0, 128),)),
        "latent_gain": jnp.clip(1.0 + 0.15 * jax.random.normal(streams_of[6], (KVR,), jnp.float32), 0.25, 1.75).astype(jnp.bfloat16),
        "latent_up": scatter_about(streams_of[7], (KVR, HEADS * (NOPE + VDIM)), KVR ** -0.5, 0.375, ((0, 128),)),
        "output_weight": scatter_about(streams_of[8], (HEADS * VDIM, D), 2 ** -0.5, 4.0, ((0, 128),)),
        "ffn_gain": jnp.clip(1.0 + 0.15 * jax.random.normal(streams_of[9], (D,), jnp.float32), 0.25, 1.75).astype(jnp.bfloat16),
        "gate_weight": scatter_about(streams_of[10], (D, FF), D ** -0.5, 0.125, ((0, 128),)),
        "up_weight": scatter_about(streams_of[11], (D, FF), D ** -0.5, 0.125, ((0, 128),)),
        "down_weight": scatter_about(streams_of[12], (FF, D), (max(FF // 64, 1)) ** -0.5, 0.625, ((0, 128),)),
        "cotangent": scatter_about(streams_of[13], (TOKENS, D), 1.0, 6.0, ((0, 128),)),
    }


@jax.custom_vjp
def low(v):
    return lax.optimization_barrier(v.astype(jnp.bfloat16)).astype(jnp.float32)

@jax.custom_vjp
def low_back(v):
    return v

def low_keep(v):
    return (low(v), None)

def low_pass(kept, grad):
    return (grad,)

def back_keep(v):
    return (v, None)

def back_low(kept, grad):
    return (low(grad),)
low.defvjp(low_keep, low_pass)
low_back.defvjp(back_keep, back_low)
EPS = 1e-05
RESIDUAL = 1.4 / math.sqrt(62.0)
NEGATIVE = -1e+30

def rms(value, gain):
    return value * lax.rsqrt(lax.optimization_barrier(jnp.mean(value * value, axis=-1, keepdims=True)) + EPS) * gain

def rotate(pair, cosine, sine):
    half = pair.shape[-1] // 2
    first, second = (pair[..., :half], pair[..., half:])
    return jnp.concatenate([first * cosine - second * sine, first * sine + second * cosine], axis=-1)

def project(left, matrix):
    return jnp.einsum('nle,ef->nlf', left, matrix, precision=lax.Precision.HIGHEST)

def forward(params, inputs):
    entry_gain, query_down, query_gain, query_up, latent_down, latent_gain, latent_up, output_weight, ffn_gain, gate_weight, up_weight, down_weight = params
    count = inputs.shape[0]
    place = jnp.arange(SEQ_LEN).astype(jnp.float32)
    freqs = 10000.0 ** (-2.0 * jnp.arange(ROPE // 2).astype(jnp.float32) / ROPE)
    turn = place[:, None] * freqs[None, :]
    cosine, sine = (jnp.cos(turn), jnp.sin(turn))
    normed = low(rms(inputs, entry_gain))
    query_latent = low_back(project(normed, query_down))
    query_normed = low(rms(query_latent, query_gain))
    query_full = low_back(project(query_normed, query_up)).reshape(count, SEQ_LEN, HEADS, NOPE + ROPE)
    queries = low(jnp.concatenate([query_full[..., :NOPE], rotate(query_full[..., NOPE:], cosine[:, None, :], sine[:, None, :])], axis=-1))
    latent_full = low_back(project(normed, latent_down))
    latent_normed = low(rms(latent_full[..., :KVR], latent_gain))
    key_value = low_back(project(latent_normed, latent_up)).reshape(count, SEQ_LEN, HEADS, NOPE + VDIM)
    key_rope = rotate(latent_full[..., KVR:], cosine, sine)
    keys = low(jnp.concatenate([key_value[..., :NOPE], jnp.broadcast_to(key_rope[:, :, None, :], (count, SEQ_LEN, HEADS, ROPE))], axis=-1))
    values = low(key_value[..., NOPE:])
    scores = jnp.einsum('nshd,nthd->nhst', queries, keys, precision=lax.Precision.HIGHEST)
    scores = low_back(scores * (NOPE + ROPE) ** (-0.5))
    rows = jnp.arange(SEQ_LEN)
    scores = jnp.where(rows[:, None] >= rows[None, :], scores, NEGATIVE)
    top = lax.optimization_barrier(jnp.max(scores, axis=-1, keepdims=True))
    expo = jnp.exp(scores - top)
    probs = low(expo / lax.optimization_barrier(jnp.sum(expo, axis=-1, keepdims=True)))
    attended = jnp.einsum('nhst,nthd->nshd', probs, values, precision=lax.Precision.HIGHEST)
    attended = low_back(low(attended)).reshape(count, SEQ_LEN, HEADS * VDIM)
    branch = low_back(project(attended, output_weight))
    middle = inputs + RESIDUAL * branch
    ffn_normed = low(rms(middle, ffn_gain))
    gate = low_back(project(ffn_normed, gate_weight))
    upper = low_back(project(ffn_normed, up_weight))
    hidden = low(jax.nn.silu(gate) * upper)
    ffn_branch = low_back(project(hidden, down_weight))
    return middle + RESIDUAL * ffn_branch

def reference(tokens, entry_gain, query_down, query_gain, query_up, latent_down, latent_gain, latent_up, output_weight, ffn_gain, gate_weight, up_weight, down_weight, cotangent):
    params = tuple((item.astype(jnp.float32) for item in (entry_gain, query_down, query_gain, query_up, latent_down, latent_gain, latent_up, output_weight, ffn_gain, gate_weight, up_weight, down_weight)))
    number = TOKENS // SEQ_LEN
    block = math.gcd(number, 16)
    inputs = tokens.astype(jnp.float32).reshape(number // block, block, SEQ_LEN, D)
    incoming = cotangent.astype(jnp.float32).reshape(number // block, block, SEQ_LEN, D)

    def step(total, pair):
        piece_in, piece_grad = pair
        result, pull = jax.vjp(forward, params, piece_in)
        param_grads, input_grad = pull(piece_grad)
        total = jax.tree.map(lambda left, right: left + right, total, param_grads)
        return (total, (result, input_grad))
    zeros = tuple((jnp.zeros_like(item) for item in params))
    grads, (results, input_grads) = lax.scan(step, zeros, (inputs, incoming))
    return (results.reshape(TOKENS, D).astype(jnp.bfloat16), input_grads.reshape(TOKENS, D), grads[0], grads[1], grads[2], grads[3], grads[4], grads[5], grads[6], grads[7], grads[8], grads[9], grads[10], grads[11])
```

```python
import functools
import math

import jax
import jax.numpy as jnp
import numpy as np
from jax import lax
from jax.experimental import pallas as pl
from jax.experimental.pallas import tpu as pltpu
from jax.sharding import Mesh
from jax.sharding import PartitionSpec as P

D = 2560
QR = 768
KVR = 256
HEADS = 40
NOPE = 64
ROPE = 32
VDIM = 64
FF = 6400
SEQ_LEN = 128
EPS = 1e-05
RESIDUAL = 1.4 / math.sqrt(62.0)
NEGATIVE = -1e30
SCALE = (NOPE + ROPE) ** (-0.5)

AXES = ("zh", "y", "zl", "x", "c")
SIZES = (2, 4, 2, 4, 2)
RING = ("zh", "zl")
TEAM = ("zh", "zl", "c")
SHARDS = ("y", "x")
NTEAM = 8
NSHARD = 16
LAT = 1152
MY_HEADS = HEADS // NTEAM
WIDE = MY_HEADS * 128
PADDED_FF = 896
PADDED_IN = 384

bf16 = jnp.bfloat16
f32 = jnp.float32


def dot(a, b):
    return jnp.dot(a, b, preferred_element_type=f32)


def dot_t(a, b):
    return lax.dot_general(a, b, (((1,), (1,)), ((), ())), preferred_element_type=f32)


def t_dot(a, b):
    return lax.dot_general(a, b, (((0,), (0,)), ((), ())), preferred_element_type=f32)


def up(block):
    return lax.ppermute(block, RING, [(i, (i + 1) % 4) for i in range(4)])


def down(block):
    return lax.ppermute(block, RING, [(i, (i + 3) % 4) for i in range(4)])


def across(block):
    return lax.ppermute(block, "c", [(0, 1), (1, 0)])


def opposite(block):
    pairs = [(2 * z + c, 2 * ((z + (1, 3)[c]) % 4) + c) for z in range(4) for c in range(2)]
    return lax.ppermute(block, TEAM, pairs)


def pick_kernel(core_ref, zero_ref, one_ref, out_ref):
    @pl.when(core_ref[0] == 0)
    def _():
        out_ref[...] = zero_ref[...]

    @pl.when(core_ref[0] != 0)
    def _():
        out_ref[...] = one_ref[...]


def team_near(own):
    return [own, across(own), down(own), None, None, None, up(own), None]


def team_far(blocks, early=(), later=()):
    core = lax.axis_index("c").astype(jnp.int32).reshape(1)
    above, below = blocks[2], blocks[6]
    (mine,) = call(
        pick_kernel, [(above.shape, bf16)], core, below, above, scalars=True, early=early
    )
    far = opposite(mine)
    above, below = gate(above, mine), gate(below, mine)
    blocks = [*blocks[:2], above, across(above), None, None, below, across(below)]
    if later:
        blocks_later = later(blocks)
        far = gate(far, jax.tree.leaves(blocks_later)[0])
        blocks[4:6] = far, across(far)
        return blocks, blocks_later
    blocks[4:6] = far, across(far)
    return blocks


def beyond(block):
    return lax.ppermute(block, RING, [(i, (i + 2) % 4) for i in range(4)])


def team_gather(own, *early):
    above, far, below = down(own), beyond(own), up(own)
    if early:
        above, far, below = gates([above, far, below], *early)
    return [own, across(own), above, across(above), far, across(far), below, across(below)]


def chip_sum(one, two):
    return (one.astype(f32) + across(two).astype(f32)).astype(bf16)


def team_sums(pairs):
    return [chip_sum(*pair) for pair in pairs]


def team_scatter(own, sums):
    above, far, below = sums
    return own[0], across(own[1]), up(above), beyond(far), down(below)


def ring_near(above, below, passing):
    first = (lax.axis_index("c") == 0).astype(f32)
    passed, passing = passing, passing.astype(f32)
    above = above[0].astype(f32) + across(above[1]).astype(f32) + first * passing
    below = below[0].astype(f32) + across(gate(below[1], passed)).astype(f32) + (1.0 - first) * passing
    return above.astype(bf16), below.astype(bf16)


def ring_last(own, above, below):
    above, below = up(above), down(below)
    return own[0], across(gate(own[1], above, below)), above, below


def place():
    return lax.axis_index(RING), lax.axis_index("c")


def absolute_places():
    z, c = place()
    y, x = lax.axis_index("y"), lax.axis_index("x")
    team = [(z + dz) % 4 * 2 + (c + dc) % 2 for dz in range(4) for dc in range(2)]
    shards = [(yy - y + 4) % 4 * 4 + (xx - x + 4) % 4 for yy in range(4) for xx in range(4)]
    owners = [(y + dy) % 4 * 4 + (x + dx) % 4 for dy in range(4) for dx in range(4)]
    return jnp.stack(team + shards + owners).astype(jnp.int32)


def team_exchange(blocks):
    return lax.all_to_all(blocks, TEAM, 0, 0, tiled=True)


def owner_pairs():
    pairs = []
    for zh in range(2):
        for y in range(4):
            for zl in range(2):
                for x in range(4):
                    for c in range(2):
                        source = zh * 64 + y * 16 + zl * 8 + x * 2 + c
                        yy, xx = zl * 2 + x // 2, x % 2 * 2 + c
                        target = zh * 64 + yy * 16 + (y // 2) * 8 + xx * 2 + y % 2
                        pairs.append((source, target))
    return pairs


def to_slices(block):
    return lax.ppermute(block, AXES, owner_pairs())


def to_owners(block):
    return lax.ppermute(block, AXES, [(b, a) for a, b in owner_pairs()])


def shard_gather(block):
    return lax.all_gather(block, SHARDS, axis=0, tiled=False)


def shard_scatter(blocks):
    return lax.psum_scatter(blocks, SHARDS, scatter_dimension=0, tiled=False)


def shard_spread(block, *early):
    def along(axis, rows):
        return [rows] + [
            lax.ppermute(rows, axis, [(i, (i - d) % 4) for i in range(4)]) for d in (1, 2, 3)
        ]

    return along("y", gate(jnp.concatenate(along("x", block), axis=0), *early))


def collect_step(axis, parts, steps):
    return sum(
        lax.ppermute(parts[d], axis, [(i, (i + d) % 4) for i in range(4)]).astype(f32) for d in steps
    )


def shard_collect(slabs, *early):
    rows = (slabs[0].astype(f32) + collect_step("y", slabs, (1, 2, 3))).astype(bf16)
    rows = gate(rows, *early)
    return rows[0].astype(f32) + collect_step("x", rows, (1, 2, 3))


def shard_sum(blocks):
    return jnp.sum(lax.all_to_all(blocks, SHARDS, 0, 0, tiled=True).astype(f32), axis=0)


def gates(late, *early):
    return pl.pallas_call(
        lambda *refs: None,
        in_specs=[pl.BlockSpec(memory_space=pl.ANY)] * (len(late) + len(early)),
        out_specs=[pl.BlockSpec(memory_space=pl.ANY)] * len(late),
        out_shape=[jax.ShapeDtypeStruct(one.shape, one.dtype) for one in late],
        input_output_aliases={i: i for i in range(len(late))},
        cost_estimate=pl.CostEstimate(flops=0, bytes_accessed=0, transcendentals=0),
    )(*late, *early)


def gate(late, *early):
    return gates([late], *early)[0]


def selection(rows, cols, pairs):
    matrix = np.zeros((rows, cols), np.float32)
    for row, col, value in pairs:
        matrix[row, col] = value
    return jnp.asarray(matrix.astype(jnp.bfloat16))


def row_order(quarters):
    pairs = []
    for new in range(1024):
        block, j = divmod(new, 6) if new < QR else divmod(new - QR, 2)
        j = j if new < QR else 6 + j
        zh, y, zl, x, c = block // 64, block // 16 % 4, block // 8 % 2, block // 2 % 4, block % 2
        old = ((((y * 4 + x) * 2 + zh) * 2 + zl) * 2 + c) * 8 + j
        pairs.append((new, old % 4 * 256 + old // 4 if quarters else old, 1.0))
    return selection(1024, 1024, pairs)


def head_rows():
    rows = range(MY_HEADS * VDIM)
    return selection(
        WIDE, PADDED_IN, [(r // VDIM * 128 + NOPE + r % VDIM, r // 20 * 24 + r % 20, 1.0) for r in rows]
    )


def spread():
    pairs = []
    for new in range(WIDE):
        head, lane = divmod(new, 128)
        j = lane - 96
        if j < 0:
            pairs.append((head * 96 + lane, new, 1.0))
        else:
            pairs.append((head * 96 + 64 + (j + 16) % 32, new, -1.0 if j < 16 else 1.0))
    return selection(WIDE, WIDE, pairs)


def rope_keys():
    lanes = [lane for lane in range(WIDE) if lane % 128 >= NOPE]
    return selection(128, WIDE, [(lane % 32, lane, 1.0) for lane in lanes])


GATHERED = [((zh * 4 + y) * 2 + zl) * 4 + x for y in range(4) for x in range(4) for zh in range(2) for zl in range(2)]
OWNED = [GATHERED.index(i) for i in range(64)]


def reorder(rows, order):
    return jnp.concatenate([rows[:, 40 * i : 40 * i + 40] for i in order], axis=1)


def call(kernel, outs, *operands, flops=0, scalars=False, scratch=(), limit=60, early=(), left=0):
    count, skipped = len(operands), len(operands) + len(early)
    spaces = [pl.BlockSpec()] * (count - left)
    spaces += [pl.BlockSpec(memory_space=pl.ANY)] * (left + len(early))
    if scalars:
        spaces[0] = pl.BlockSpec(memory_space=pltpu.SMEM)
    outs = [jax.ShapeDtypeStruct(*out) for out in outs]

    def body(*refs):
        kernel(*refs[:count], *refs[skipped:])

    moved = sum(one.size * one.dtype.itemsize for one in (*operands, *outs))
    return pl.pallas_call(
        body,
        in_specs=spaces,
        out_shape=outs,
        scratch_shapes=list(scratch),
        compiler_params=pltpu.CompilerParams(vmem_limit_bytes=limit * 2**20),
        cost_estimate=pl.CostEstimate(flops=int(flops), bytes_accessed=moved, transcendentals=0),
    )(*operands, *early)


def total(refs):
    return sum(ref[...].astype(f32) for ref in refs)


HIDDEN_SHARDS = [(t, i) for t in range(NTEAM) for i in range(NSHARD)]
UNIT_ROWS = 3 * SEQ_LEN
PACKED_ROWS = UNIT_ROWS + 14 * 24


def entry_kernel(tokens_ref, gate_ref, upper_ref, gain_ref, sent_ref):
    value = tokens_ref[...].astype(f32)
    unit = value * inverse_rms(value)
    gap = jnp.zeros((SEQ_LEN, 4), f32)
    weights = [ref[...].astype(f32) * gain_ref[...] for ref in (gate_ref, upper_ref)]
    wide_gap, low_gap = jnp.zeros((20, 6), f32), jnp.zeros((4, 2 * PADDED_FF), f32)
    for t in range(NTEAM):
        zh, zl, c = t // 4, t // 2 % 2, t % 2
        columns = []
        for y in range(4):
            for x in range(4):
                at = 20 * ((((zh * 4 + y) * 2 + zl) * 4 + x) * 2 + c)
                columns += [unit[:, at : at + 20], gap]
        mine = jnp.concatenate(columns, axis=1).astype(bf16)
        for k in range(3):
            sent_ref[t, SEQ_LEN * k : SEQ_LEN * (k + 1), :] = mine[:, 128 * k : 128 * (k + 1)]
        columns = []
        for weight in weights:
            for i in range(NSHARD):
                at = 800 * t + 50 * i
                columns += [weight[:, at : at + 50], wide_gap]
        mine = jnp.concatenate([jnp.concatenate(columns, axis=1), low_gap], axis=0)
        mine = jnp.concatenate([mine[:, 128 * k : 128 * (k + 1)] for k in range(14)], axis=0)
        sent_ref[t, UNIT_ROWS:, :] = mine.astype(bf16)


def unit_of(received_ref, t):
    return jnp.concatenate(
        [received_ref[t, SEQ_LEN * k : SEQ_LEN * (k + 1), :] for k in range(3)], axis=1
    )


def wide_kernel(received_ref, out_ref):
    rows = []
    for t in range(NTEAM):
        mine = received_ref[t, UNIT_ROWS:, :].astype(f32)
        rows.append(jnp.concatenate([mine[24 * k : 24 * k + 20] for k in range(14)], axis=1))
    out_ref[...] = jnp.concatenate(rows, axis=0).astype(bf16)


def wide_back_kernel(received_ref, gate_ref, upper_ref, gain_ref, gate_out, upper_out, gain_out):
    gain_grad = jnp.zeros((20, 1), f32)
    for weight_ref, out_ref, base in ((gate_ref, gate_out, 0), (upper_ref, upper_out, PADDED_FF)):
        received = [received_ref[t].astype(f32) for t in range(NTEAM)]
        grad = jnp.concatenate(
            [received[t][:, base + 56 * i : base + 56 * i + 50] for t, i in HIDDEN_SHARDS], axis=1
        )
        gain_grad += jnp.sum(grad * weight_ref[...].astype(f32), axis=1, keepdims=True)
        out_ref[...] = gain_ref[...] * grad
    gain_out[...] = gain_grad


def latent_kernel(places_ref, units_ref, *refs):
    downs_refs, outs, downs_ref, held = refs[:4], refs[4:12], refs[12], refs[13]
    for dy in range(4):
        slab = downs_refs[dy][...].astype(f32)
        for dx in range(4):
            held[4 * dy + dx] = slab[24 * dx : 24 * dx + 24]
    downs = jnp.concatenate([held[places_ref[NTEAM + i]] for i in range(NSHARD)], axis=0).astype(bf16)
    downs_ref[...] = downs
    for i in range(NTEAM):
        outs[i][...] = dot(unit_of(units_ref, places_ref[i]), downs).astype(bf16)


def latent_back_kernel(places_ref, units_ref, downs_ref, *refs):
    grad_refs, slabs, unit_grad_ref, held = refs[:8], refs[8:12], refs[12], refs[13]
    units = jnp.concatenate([unit_of(units_ref, places_ref[i]) for i in range(NTEAM)], axis=0)
    grads = jnp.concatenate([ref[...] for ref in grad_refs], axis=0)
    rows = t_dot(units, grads)
    for i in range(NSHARD):
        held[i] = rows[24 * i : 24 * i + 24]
    for dy in range(4):
        for dx in range(4):
            slabs[dy][dx] = held[places_ref[NTEAM + NSHARD + 4 * dy + dx]].astype(bf16)
    downs = downs_ref[...]
    for i in range(NTEAM):
        unit_grad_ref[places_ref[i]] = dot_t(grad_refs[i][...], downs).astype(bf16)


def swapped(rope):
    return jnp.concatenate([-rope[:, 16:32], rope[:, :16], rope[:, 32:]], axis=1)


def packing_kernel(*refs):
    cosine_ref, sine_ref, latent_ref, packed_ref = refs[5:]
    latent = total(refs[:5])
    latent_ref[...] = latent
    query, part, rope = latent[:, :QR], latent[:, QR : QR + KVR], latent[:, QR + KVR :]
    packed_ref[:, :QR] = (query * inverse_rms(query)).astype(bf16)
    packed_ref[:, QR : QR + KVR] = (part * inverse_rms(part)).astype(bf16)
    packed_ref[:, QR + KVR :] = (rope * cosine_ref[...] + swapped(rope) * sine_ref[...]).astype(bf16)


def packing_back_kernel(*refs):
    latent_ref, cosine_ref, sine_ref, out_ref = refs[5:]
    grad = total(refs[:5])
    latent = latent_ref[...]
    for at in (slice(0, QR), slice(QR, QR + KVR)):
        value = latent[:, at]
        out_ref[:, at] = norm_back(value, inverse_rms(value), grad[:, at]).astype(bf16)
    rope = grad[:, QR + KVR :]
    out_ref[:, QR + KVR :] = (rope * cosine_ref[...] - swapped(rope) * sine_ref[...]).astype(bf16)


def scale_kernel(cotangent_ref, out_ref):
    out_ref[...] = (RESIDUAL * cotangent_ref[...].astype(f32)).astype(bf16)


def block_out_kernel(*refs):
    *parts, middle_ref, out_ref = refs
    out_ref[...] = (middle_ref[...] + RESIDUAL * total(parts)).astype(bf16)


def middle_kernel(*refs):
    *parts, tokens_ref, middle_ref, unit_ref = refs
    middle = tokens_ref[...].astype(f32) + RESIDUAL * total(parts)
    middle_ref[...] = middle
    unit_ref[...] = reorder(middle * inverse_rms(middle), GATHERED).astype(bf16)


def middle_back_kernel(*refs):
    middle_ref, cotangent_ref, grad_ref, branch_ref = refs[5:]
    scaled = reorder(total(refs[:5]), OWNED)
    middle = middle_ref[...]
    grad = cotangent_ref[...].astype(f32) + norm_back(middle, inverse_rms(middle), scaled)
    grad_ref[...] = grad
    branch_ref[...] = (RESIDUAL * grad).astype(bf16)


def finish_kernel(unit_grad_ref, tokens_ref, middle_grad_ref, out_ref):
    columns = []
    for b in range(128):
        zh, y, zl, x, c = b // 64, b // 16 % 4, b // 8 % 2, b // 2 % 4, b % 2
        at = 24 * (4 * y + x)
        columns.append(unit_grad_ref[zh * 4 + zl * 2 + c].astype(f32)[:, at : at + 20])
    scaled = jnp.concatenate(columns, axis=1)
    value = tokens_ref[...].astype(f32)
    out_ref[...] = middle_grad_ref[...] + norm_back(value, inverse_rms(value), scaled)


FFN_STEPS = 2


def rows_of(refs):
    return jnp.concatenate([ref[...] for ref in refs], axis=0)


def ffn_kernel(pairs, *refs):
    count = 2 * pairs
    ins, backs, refs = refs[:count], refs[count : 2 * count], refs[2 * count :]
    wide_ref, down_ref, outs, (wide, down_rows, wide_sems, down_sem) = refs[0], refs[1], refs[2:-4], refs[-4:]
    step = D // FFN_STEPS
    copies = [
        pltpu.make_async_copy(
            wide_ref.at[pl.ds(k * step, step)], wide.at[pl.ds(k * step, step)], wide_sems.at[k]
        )
        for k in range(FFN_STEPS)
    ]
    last = pltpu.make_async_copy(down_ref, down_rows, down_sem)
    for copy in (*copies, last):
        copy.start()
    entering = rows_of(ins)
    gate_up = jnp.zeros((count * SEQ_LEN, 2 * PADDED_FF), f32)
    for k, copy in enumerate(copies):
        copy.wait()
        gate_up += dot(entering[:, k * step : (k + 1) * step], wide[k * step : (k + 1) * step])
    last.wait()
    hidden_grad = dot_t(rows_of(backs), down_rows[...])
    gate, upper = gate_up[:, :PADDED_FF], gate_up[:, PADDED_FF:]
    sigma = jax.nn.sigmoid(gate)
    swish = gate * sigma
    hidden = (swish * upper).astype(bf16)
    gate_grad = (hidden_grad * upper * (sigma + swish * (1.0 - sigma))).astype(bf16)
    both = jnp.concatenate([gate_grad, (hidden_grad * swish).astype(bf16)], axis=1)
    width = dot_t(both, wide[...]).astype(bf16)
    for i in range(pairs):
        start = 2 * SEQ_LEN * i
        middle, stop = start + SEQ_LEN, start + 2 * SEQ_LEN
        both_ref, hidden_ref, one_ref, two_ref = outs[4 * i : 4 * i + 4]
        both_ref[...], hidden_ref[...] = both[start:stop], hidden[start:stop]
        one_ref[...], two_ref[...] = width[start:middle], width[middle:stop]


def ffn_out_kernel(*refs):
    down_rows = refs[4][...]
    for i in range(4):
        part = dot(refs[i][...], down_rows).astype(bf16)
        refs[5 + 2 * i][...], refs[6 + 2 * i][...] = part[:SEQ_LEN], part[SEQ_LEN:]


def grouped(flat, size):
    return [flat[i : i + size] for i in range(0, len(flat), size)]


def ffn(ins, backs, wide, down_rows, *early):
    pairs, rows, block = len(ins) // 2, 2 * SEQ_LEN, ((SEQ_LEN, D), bf16)
    outs = call(
        functools.partial(ffn_kernel, pairs),
        [((rows, 2 * PADDED_FF), bf16), ((rows, PADDED_FF), bf16), block, block] * pairs,
        *ins, *backs, wide, down_rows,
        flops=2 * pairs * rows * D * 5 * PADDED_FF, early=early, left=2,
        scratch=[
            pltpu.VMEM((D, 2 * PADDED_FF), bf16), pltpu.VMEM((PADDED_FF, D), bf16),
            pltpu.SemaphoreType.DMA((FFN_STEPS,)), pltpu.SemaphoreType.DMA(()),
        ],
    )
    return grouped(outs, 4)


def slices_kernel(slices_ref, rows_ref, heads_ref, spread_ref, tail_ref, wq_ref, wk_ref, wv_ref, wo_ref, down_ref):
    for i in range(NSHARD):
        down_ref[56 * i : 56 * (i + 1), :] = slices_ref[i, 24:80, :]
    out_rows = jnp.concatenate([slices_ref[i, :24, :].astype(f32) for i in range(NSHARD)], axis=0)
    wo_ref[...] = dot(heads_ref[...], out_rows.astype(bf16)).astype(bf16)
    ups = jnp.concatenate(
        [slices_ref[i, 80:, 640 * k : 640 * (k + 1)] for k in range(4) for i in range(NSHARD)], axis=0
    )
    ups = dot(rows_ref[...], ups).astype(bf16)
    wq_ref[...] = dot(ups[:QR], spread_ref[...]).astype(bf16)
    latent = ups[QR:]
    is_key = lax.broadcasted_iota(jnp.int32, latent.shape, 1) % 128 < NOPE
    wv_ref[...] = jnp.where(is_key, jnp.zeros_like(latent), latent)
    wk_ref[:KVR, :] = jnp.where(is_key, latent, jnp.zeros_like(latent))
    wk_ref[KVR:, :] = tail_ref[...]


def heads_grad_kernel(places_ref, *refs):
    attended_refs, grad_refs, (rows_ref, spread_ref) = refs[:4], refs[4:12], refs[12:14]
    wq_refs, wl_refs, slabs, held = refs[14:17], refs[17:20], refs[20:24], refs[24]
    out_rows = t_dot(rows_of(attended_refs), rows_of(grad_refs))
    grad = jnp.concatenate(
        [dot_t(total(wq_refs).astype(bf16), spread_ref[...]).astype(bf16), total(wl_refs).astype(bf16)], axis=0
    )
    rows = t_dot(rows_ref[...], grad)
    for i in range(NSHARD):
        quarters = [rows[256 * k + 16 * i : 256 * k + 16 * i + 16] for k in range(4)]
        held[i, :24, :] = out_rows[24 * i : 24 * i + 24]
        held[i, 24:, :] = jnp.concatenate(quarters, axis=1)
    for dy in range(4):
        for dx in range(4):
            slabs[dy][dx] = held[places_ref[NTEAM + NSHARD + 4 * dy + dx]].astype(bf16)


def angles():
    place_in = lax.broadcasted_iota(jnp.int32, (SEQ_LEN, ROPE // 2), 0).astype(f32)
    freqs = 10000.0 ** (-2.0 * lax.broadcasted_iota(jnp.int32, (SEQ_LEN, ROPE // 2), 1).astype(f32) / ROPE)
    turn = place_in * freqs
    return jnp.cos(turn), jnp.sin(turn)


def mask_and_scale(q, k):
    scores = dot_t(q, k) * SCALE
    rows = lax.broadcasted_iota(jnp.int32, scores.shape, 0)
    cols = lax.broadcasted_iota(jnp.int32, scores.shape, 1)
    return jnp.where(rows >= cols, scores, NEGATIVE)


def softmax(scores):
    expo = jnp.exp(scores - jnp.max(scores, axis=-1, keepdims=True))
    return expo / jnp.sum(expo, axis=-1, keepdims=True)


def head_places(pairs):
    for s in range(2 * pairs):
        for h in range(MY_HEADS):
            yield slice(s * SEQ_LEN, (s + 1) * SEQ_LEN), slice(h * 128, (h + 1) * 128)


def attend_kernel(pairs, *refs):
    count = 2 * pairs
    wq_ref, wk_ref, wv_ref, wo_ref, turn_ref, rows_ref = refs[count : count + 6]
    outs, attended_ref = refs[count + 6 : -1], refs[-1]
    lat = rows_of(refs[:count])
    queries = dot(lat[:, :QR], wq_ref[...])
    keys = dot(lat[:, QR:], wk_ref[...]).astype(bf16)
    values = dot(lat[:, QR : QR + KVR], wv_ref[...]).astype(bf16)
    turn = turn_ref[...]
    for at in head_places(pairs):
        pair, start = divmod(at[0].start, 2 * SEQ_LEN)
        inner = (slice(start, start + SEQ_LEN), at[1])
        q = (queries[at] * turn).astype(bf16)
        probs = softmax(mask_and_scale(q, keys[at])).astype(bf16)
        outs[7 * pair + 3][inner] = q
        outs[7 * pair + 4][inner] = keys[at]
        outs[7 * pair + 5][inner] = values[at]
        outs[7 * pair + 6][inner] = probs
        attended_ref[at] = dot(probs, values[at]).astype(bf16)
    out_rows = dot(attended_ref[...], rows_ref[...]).astype(bf16)
    out = dot(attended_ref[...], wo_ref[...]).astype(bf16)
    for i in range(pairs):
        start = 2 * SEQ_LEN * i
        middle, stop = start + SEQ_LEN, start + 2 * SEQ_LEN
        outs[7 * i][...], outs[7 * i + 1][...] = out[start:middle], out[middle:stop]
        outs[7 * i + 2][...] = out_rows[start:stop]


def attend_back_kernel(pairs, *refs):
    count = 2 * pairs
    lat, grad = rows_of(refs[:count]), rows_of(refs[count : 2 * count])
    refs = refs[2 * count :]
    heads, (wq_ref, wk_ref, wv_ref, wo_ref, turn_ref) = refs[: 4 * pairs], refs[4 * pairs : 4 * pairs + 5]
    refs = refs[4 * pairs + 5 :]
    outs, (wq_grad_ref, wl_grad_ref, q_grad, k_grad, v_grad) = refs[:count], refs[count:]
    attended_grad = dot_t(grad, wo_ref[...]).astype(bf16)
    turn = turn_ref[...] * SCALE
    for at in head_places(pairs):
        pair, start = divmod(at[0].start, 2 * SEQ_LEN)
        inner = (slice(start, start + SEQ_LEN), at[1])
        queries, keys, values, probs_low = (ref[inner] for ref in heads[4 * pair : 4 * pair + 4])
        probs = probs_low.astype(f32)
        probs_grad = dot_t(attended_grad[at], values)
        mean = jnp.sum(probs * probs_grad, axis=-1, keepdims=True)
        scores_grad = (probs * (probs_grad - mean)).astype(bf16)
        q_grad[at] = (dot(scores_grad, keys) * turn).astype(bf16)
        k_grad[at] = (t_dot(scores_grad, queries) * SCALE).astype(bf16)
        v_grad[at] = t_dot(probs_low, attended_grad[at]).astype(bf16)
    lane = lax.broadcasted_iota(jnp.int32, k_grad.shape, 1)
    kv_grad = jnp.where(lane % 128 < NOPE, k_grad[...], v_grad[...])
    key_side = dot_t(k_grad[...], wk_ref[...])
    value_side = dot_t(v_grad[...], wv_ref[...])
    query_side = dot_t(q_grad[...], wq_ref[...])
    for i, out in enumerate(outs):
        at = slice(SEQ_LEN * i, SEQ_LEN * (i + 1))
        out[:, :QR] = query_side[at].astype(bf16)
        out[:, QR : QR + KVR] = (key_side[at, :KVR] + value_side[at]).astype(bf16)
        out[:, QR + KVR :] = key_side[at, KVR:].astype(bf16)
    wq_grad_ref[...] = t_dot(lat[:, :QR], q_grad[...]).astype(bf16)
    wl_grad_ref[...] = t_dot(lat[:, QR : QR + KVR], kv_grad).astype(bf16)


def whole(shape):
    return pl.BlockSpec(shape, lambda i: (0,) * len(shape))


def attend(blocks, *weights, early=()):
    pairs, rows, block = len(blocks) // 2, 2 * SEQ_LEN, ((SEQ_LEN, D), bf16)
    outs = call(
        functools.partial(attend_kernel, pairs),
        [block, block, ((rows, PADDED_IN), bf16), *([((rows, WIDE), bf16)] * 4)] * pairs,
        *blocks, *weights,
        flops=2 * pairs * rows * (QR * WIDE + 640 * WIDE + WIDE * D + 512 * WIDE),
        scratch=[pltpu.VMEM((pairs * rows, WIDE), bf16)], early=early,
    )
    return grouped(outs, 7)


def attend_back(blocks, grads, heads, weights, early=()):
    pairs, rows = len(blocks) // 2, 2 * SEQ_LEN
    *outs, wq_grad, wl_grad = call(
        functools.partial(attend_back_kernel, pairs),
        [*([((SEQ_LEN, LAT), bf16)] * 2 * pairs), ((QR, WIDE), bf16), ((KVR, WIDE), bf16)],
        *blocks, *grads, *(one for head in heads for one in head[3:]), *weights,
        flops=2 * pairs * rows * (2 * QR * WIDE + 900 * WIDE + WIDE * D + 512 * WIDE),
        scratch=[pltpu.VMEM((pairs * rows, WIDE), bf16)] * 3, early=early,
    )
    return grouped(outs, 2), wq_grad, wl_grad


def ffn_grads_kernel(*refs):
    refs = (*refs[:24], refs[-1])
    ins, backs, boths, hiddens, out_ref = refs[:8], refs[8:16], refs[16:20], refs[20:24], refs[24]
    step = pl.program_id(0)
    left = jnp.concatenate([ref[...] for ref in ins], axis=0)
    wide = t_dot(left, jnp.concatenate([ref[...] for ref in boths], axis=0)).astype(bf16)
    for i in range(4):
        out_ref[i, :160, :] = wide[160 * i : 160 * (i + 1)]
    right = jnp.concatenate([ref[...] for ref in backs], axis=0)

    for now in range(4):

        @pl.when(step == now)
        def _():
            at = slice(224 * now, 224 * (now + 1))
            rows = t_dot(jnp.concatenate([ref[:, at] for ref in hiddens], axis=0), right)
            for i in range(4):
                block = rows[56 * i : 56 * (i + 1)]
                rest = [
                    jnp.concatenate(
                        [block[8 * g : 8 * g + 8, 1792 + 256 * k : 2048 + 256 * k] for g in range(7)], axis=1
                    )
                    for k in range(3)
                ]
                out_ref[i, 160:, :] = jnp.concatenate([block[:, :1792], *rest], axis=0).astype(bf16)


def ffn_grads_of(ins, backs, boths, hiddens, *early):
    rows = 2 * SEQ_LEN
    return pl.pallas_call(
        ffn_grads_kernel,
        grid=(4,),
        in_specs=[pl.BlockSpec((SEQ_LEN, 640), lambda i: (0, i))] * 8
        + [whole((SEQ_LEN, D))] * 8
        + [whole((rows, 2 * PADDED_FF))] * 4
        + [whole((rows, PADDED_FF))] * 4
        + [pl.BlockSpec(memory_space=pl.ANY)] * len(early),
        out_specs=pl.BlockSpec((4, 240, 2 * PADDED_FF), lambda i: (i, 0, 0)),
        out_shape=jax.ShapeDtypeStruct((NSHARD, 240, 2 * PADDED_FF), bf16),
        compiler_params=pltpu.CompilerParams(vmem_limit_bytes=60 * 1024 * 1024),
        cost_estimate=pl.CostEstimate(
            flops=2 * 1024 * D * 3 * PADDED_FF, bytes_accessed=36 * 2**20, transcendentals=0
        ),
    )(*ins, *backs, *boths, *hiddens, *early)


def unpack_down(block):
    rest = block[56:].reshape(3, 8, 7, 256).transpose(2, 1, 0, 3).reshape(56, 768)
    return jnp.concatenate([block[:56], rest], axis=1)


def inverse_rms(value):
    return lax.rsqrt(jnp.mean(value * value, axis=-1, keepdims=True) + EPS)


def norm_back(value, factor, scaled):
    return factor * scaled - value * factor**3 * jnp.mean(scaled * value, axis=-1, keepdims=True)


def on_device(
    tokens,
    entry_gain,
    query_down,
    query_gain,
    query_up,
    latent_down,
    latent_gain,
    latent_up,
    output_weight,
    ffn_gain,
    gate_weight,
    up_weight,
    down_weight,
    cotangent,
):
    count = tokens.shape[0]
    gain_0 = entry_gain.astype(f32)[:, None]
    gain_q = query_gain.astype(f32)[:, None]
    gain_l = latent_gain.astype(f32)[:, None]
    gain_1 = ffn_gain.astype(f32)[:, None]
    downs = jnp.concatenate([query_down, latent_down], axis=1).astype(f32)

    places = absolute_places()
    cosine, sine = angles()
    turn = jnp.concatenate([jnp.ones((SEQ_LEN, NOPE), f32), cosine, cosine, sine, sine], axis=1)
    rest = jnp.zeros((SEQ_LEN, 128 - ROPE), f32)
    cosine = jnp.concatenate([cosine, cosine, rest], axis=1)
    sine = jnp.concatenate([sine, sine, rest], axis=1)

    with jax.named_scope("slices"):
        ups = jnp.concatenate(
            [
                jnp.pad(
                    (gain_q * query_up.astype(f32)).astype(bf16).reshape(6, NTEAM, 480),
                    ((0, 0), (0, 0), (0, 160)),
                ),
                (gain_l * latent_up.astype(f32)).astype(bf16).reshape(2, NTEAM, 640),
            ],
            axis=0,
        )
        ups = team_exchange(ups.transpose(1, 0, 2))
        sliced = jnp.concatenate(
            [jnp.pad(output_weight, ((0, 4), (0, 0))), jnp.pad(down_weight, ((0, 6), (0, 0)))]
        )
        sliced = to_slices(sliced)
        slices = shard_gather(jnp.concatenate([sliced, ups.reshape(16, D)], axis=0))
        in_heads = head_rows()
        spread_in = spread()

    with jax.named_scope("entry"):
        my_downs = jnp.pad((gain_0 * downs).astype(bf16), ((0, 4), (0, LAT - 1056)))
        my_downs = shard_spread(my_downs, ups)
        (sent,) = call(
            entry_kernel, [((NTEAM, PACKED_ROWS, 128), bf16)], tokens, gate_weight, up_weight, gain_1, early=(ups,)
        )
        units = team_exchange(sent)
        *latent, my_downs = call(
            latent_kernel,
            [((SEQ_LEN, LAT), bf16)] * NTEAM + [((PADDED_IN, LAT), bf16)],
            places, units, *my_downs,
            flops=2 * 1024 * PADDED_IN * LAT, scalars=True, scratch=[pltpu.VMEM((NSHARD, 24, LAT), f32)],
        )
        (wide,) = call(wide_kernel, [((160, 2 * PADDED_FF), bf16)], units, early=(my_downs,))
        latent = grouped(latent, 2)
        sums = team_sums(latent[1:])
        latent, packed = call(
            packing_kernel,
            [((SEQ_LEN, LAT), f32), ((SEQ_LEN, LAT), bf16)],
            *team_scatter(latent[0], sums), cosine, sine,
        )
        wq, wk, wv, wo, down_rows = call(
            slices_kernel,
            [((QR, WIDE), bf16), ((LAT - QR, WIDE), bf16), ((KVR, WIDE), bf16), ((WIDE, D), bf16),
             ((PADDED_FF, D), bf16)],
            slices, row_order(True), in_heads, spread_in, rope_keys(),
            flops=2 * WIDE * (PADDED_IN * D + 1024 * 1024 + QR * WIDE),
        )
        weights = (wq, wk, wv, wo, turn)
        (back_in,) = call(scale_kernel, [((SEQ_LEN, D), bf16)], cotangent, early=sums)
        back_in = team_near(back_in)
        lat = team_gather(packed, wq, back_in[2], back_in[6])

    with jax.named_scope("ffn_weights"):
        wide = shard_gather(wide)
        wide = wide.reshape(D, 2 * PADDED_FF)

    with jax.named_scope("attention"):
        back_in = team_far(back_in, lat[4:5])
        (far,) = attend(lat[4:6], *weights, in_heads, early=(back_in[2], back_in[6]))
        far_sum = chip_sum(*far[:2])
        above, below = attend([*lat[2:4], *lat[6:]], *weights, in_heads, early=(far_sum,))
        near = ring_near(above[:2], below[:2], opposite(far_sum))
        (own,) = attend(lat[:2], *weights, in_heads, early=(*near, back_in[4]))
        heads = [own, above, far, below]
        middle, middle_unit = call(
            middle_kernel,
            [((SEQ_LEN, D), f32), ((SEQ_LEN, D), bf16)],
            *ring_last(own[:2], *near), tokens,
        )

    with jax.named_scope("ffn"):
        ins = team_near(middle_unit)
        (own,) = ffn(ins[:2], back_in[:2], wide, down_rows)

        def sides(blocks):
            return ffn([*blocks[2:4], *blocks[6:]], [*back_in[2:4], *back_in[6:]], wide, down_rows)

        ins, (above, below) = team_far(ins, own[:1], sides)
        (far,) = ffn(ins[4:6], back_in[4:6], wide, down_rows)
        parts = [own, above, far, below]
        boths, hiddens = ([part[i] for part in parts] for i in range(2))
        ffn_grads = ffn_grads_of(ins, back_in, boths, hiddens)
        scaled_1 = team_scatter(own[2:], team_sums([above[2:], far[2:], below[2:]]))

    with jax.named_scope("middle_back"):
        middle_grad, branch_grad = call(
            middle_back_kernel,
            [((SEQ_LEN, D), f32), ((SEQ_LEN, D), bf16)],
            *scaled_1, middle, cotangent, early=(ffn_grads,),
        )

    with jax.named_scope("attention_back"):
        grads = team_near(branch_grad)
        (own,), *own_sums = attend_back(lat[:2], grads[:2], heads[:1], weights)

        def back_sides(blocks):
            at = (2, 3, 6, 7)
            return attend_back([lat[i] for i in at], [blocks[i] for i in at], heads[1::2], weights)

        ffn_parts = call(
            ffn_out_kernel, [((SEQ_LEN, D), bf16)] * NTEAM, *hiddens, down_rows,
            flops=2 * 1024 * D * PADDED_FF, early=(branch_grad,),
        )
        grads, ((above, below), *side_sums) = team_far(grads, (own[0], ffn_parts[0]), back_sides)
        (far,), *far_sums = attend_back(lat[4:6], grads[4:6], heads[2:3], weights)
        slabs = call(
            heads_grad_kernel, [((4, 40, D), bf16)] * 4,
            places, *(head[2] for head in heads), *grads, row_order(True), spread_in,
            own_sums[0], side_sums[0], far_sums[0], own_sums[1], side_sums[1], far_sums[1],
            flops=2 * WIDE * (QR * WIDE + 1024 * 1024) + 2 * 1024 * PADDED_IN * D, scalars=True,
            scratch=[pltpu.VMEM((NSHARD, 40, D), f32)],
        )
        packed_grad = team_scatter(own, team_sums([above, far, below]))

    with jax.named_scope("latent_back"):
        (latent_grad,) = call(
            packing_back_kernel, [((SEQ_LEN, LAT), bf16)], *packed_grad, latent, cosine, sine, early=slabs[1:2]
        )
        team_grads = team_gather(latent_grad)
        first_step = slabs[0].astype(f32) + collect_step("y", dict(zip((1, 3), gates(slabs[1::2], latent_grad))), (1, 3))
        *downs_slabs, unit_grad = call(
            latent_back_kernel,
            [((4, 24, LAT), bf16)] * 4 + [((NTEAM, SEQ_LEN, PADDED_IN), bf16)],
            places, units, my_downs, *team_grads,
            flops=4 * 1024 * PADDED_IN * LAT, scalars=True, scratch=[pltpu.VMEM((NSHARD, 24, LAT), f32)],
        )
        unit_back = team_exchange(unit_grad)
        with jax.named_scope("block_out"):
            ffn_parts = grouped(gates(ffn_parts, unit_grad), 2)
            ffn_branch = team_scatter(ffn_parts[0], team_sums(ffn_parts[1:]))
        downs_grad = shard_collect(gates(downs_slabs, first_step), unit_back)[:20, :1056]
        entry_gain_grad = jnp.sum(downs_grad * downs, axis=1)
        downs_grad = gain_0 * downs_grad
        (tokens_grad,) = call(
            finish_kernel, [((SEQ_LEN, D), f32)], unit_back, tokens, middle_grad
        )

    with jax.named_scope("ffn_weight_sums"):
        ffn_grads = lax.psum_scatter(
            gate(ffn_grads, branch_grad).reshape(NSHARD * 240, 2 * PADDED_FF),
            SHARDS, scatter_dimension=0, tiled=True,
        )
        wide_grad = team_exchange(gate(ffn_grads[:160].reshape(NTEAM, 20, 2 * PADDED_FF), unit_back))
        gate_weight_grad, up_weight_grad, ffn_gain_grad = call(
            wide_back_kernel,
            [((20, FF), f32), ((20, FF), f32), ((20, 1), f32)],
            wide_grad, gate_weight, up_weight, gain_1,
        )
        ffn_gain_grad = ffn_gain_grad[:, 0]
        down_weight_grad = to_owners(unpack_down(ffn_grads[160:]))[:50].astype(f32)

        (block_out,) = call(
            block_out_kernel, [((SEQ_LEN, D), bf16)], *ffn_branch, middle, early=(wide_grad,)
        )

    with jax.named_scope("ups_sums"):
        heads_grad = first_step + collect_step("y", {2: gate(slabs[2], first_step, unit_grad)}, (2,))
        heads_grad = heads_grad.astype(bf16)
        heads_grad = (heads_grad[0].astype(f32) + collect_step("x", heads_grad, (1, 2, 3))).astype(bf16)
        output_weight_grad = to_owners(heads_grad[:24])[:20].astype(f32)
        ups_grad = team_exchange(gate(heads_grad[24:].reshape(NTEAM, 8, 640), wide_grad))
        ups_grad = ups_grad.transpose(1, 0, 2).astype(f32)
        query_sum = ups_grad[:6, :, :480].reshape(6, NTEAM * 480)
        latent_sum = ups_grad[6:].reshape(2, NTEAM * 640)
        query_gain_grad = jnp.sum(query_sum * query_up.astype(f32), axis=1)
        latent_gain_grad = jnp.sum(latent_sum * latent_up.astype(f32), axis=1)
        query_up_grad = gain_q * query_sum
        latent_up_grad = gain_l * latent_sum

    return (
        block_out,
        tokens_grad,
        entry_gain_grad,
        downs_grad[:, :QR],
        query_gain_grad,
        query_up_grad,
        downs_grad[:, QR:],
        latent_gain_grad,
        latent_up_grad,
        output_weight_grad,
        ffn_gain_grad,
        gate_weight_grad,
        up_weight_grad,
        down_weight_grad,
    )


def solution(mesh):
    apart = Mesh(mesh.devices.reshape(SIZES), AXES)
    two, one = P(AXES, None), P(AXES)
    return jax.shard_map(
        on_device,
        mesh=apart,
        in_specs=(two, one, two, one, two, two, one, two, two, one, two, two, two, two),
        out_specs=(two, two, one, two, one, two, two, one, two, two, one, two, two, two),
        check_vma=False,
    )
```
